32 devices in a mesh: dom: 32 (over z, y, x, core).
Axes of the slice: x: 2, y: 2, z: 4, core: 2. Of those that a mesh axis runs over, the one named last changes fastest.
Arguments:
- velocity: bfloat16 [3, 512, 16384], P(None, None, 'dom'), may hold values from -1.1953125 to 1.1953125
- inverse_sizes: float32 [3, 16384], P(None, 'dom'), may hold values from 0.5 to 2
- resample_x: float32 [2, 8, 8, 16384], P(None, None, None, 'dom'), may hold values from 0 to 0.25
- resample_y: float32 [2, 4, 8, 16384], P(None, None, None, 'dom'), may hold values from 0 to 0.25
- resample_z: float32 [2, 4, 8, 16384], P(None, None, None, 'dom'), may hold values from 0 to 0.25
- piece_target: int32 [2, 16384], P(None, 'dom'), may hold values from 0 to 511, as said below
- target_brick: int32 [16384, 1], P('dom'), may hold values from 0 to 31; in each aligned block of 512 rows (0 to 511, 512 to 1023, ...) at most 64 rows name the same one
- target_block: int32 [16384], P('dom'), may hold values from 0 to 2047
- brick_home: int32 [32], replicated, may hold values from 0 to 31, each once
Outputs:
- bricks: float32 [32, 2048, 128], P('dom')
The draws below stay inside these ranges and needn't reach their ends.
Inputs may be any that keep to these rules, and one draw needn't show every extreme that they name: `piece_target`: among the 2 x 512 entries of one device's columns every value appears exactly twice. `target_brick`: in the rows of one device no brick is named more than 64 times, and in some device's rows some brick is named exactly 64 times. `brick_home`: every device is the home of exactly one brick.
All inputs are finite; a program needn't handle non-finite values.
Results may differ from the reference program's by a relative error of at most 0.0023.
Values sent between devices are 32-bit elements; how exact they have to be, the bound alone decides.
No kernel may reach another device: no remote copies, remote signals or barrier semaphores. Data moves between devices by JAX's collectives and lax.ppermute only.
A program may use at most 192 MiB of HBM per device.

```python
import math
import jax
import jax.numpy as jnp
import numpy as np
from jax import lax

LAYERS = 4
EYN = 8
EZN = 16
CROSS = 128
E_DEV = 512
ELEMS = 16384
NBRICKS = 32
BLOCKS = 2048
CAPT = 64


def draw_piece_target(key, part):
    per_dev = LAYERS * EYN * EZN
    devices = ELEMS // per_dev
    subkeys = jax.random.split(key, devices)

    def shuffled(single):
        return jax.random.permutation(single, 2 * per_dev)
    orders = jax.vmap(shuffled)(subkeys)
    targets = (orders // 2).astype(jnp.int32).reshape(devices, per_dev, 2)
    return jnp.transpose(targets, (2, 0, 1)).reshape(2, ELEMS)


def with_ends(values, key, low, top_value):
    longest = values.shape.index(max(values.shape))
    spots = []
    for shift in (0, 1):
        where = [jax.random.randint(jax.random.fold_in(key, axis), (), 0, length) for axis, length in enumerate(values.shape)]
        where[longest] = (where[longest] + shift) % values.shape[longest]
        spots.append(tuple(where))
    return values.at[spots[0]].set(low).at[spots[1]].set(top_value)


def block_levels(stream_key, dims, cuts, low, high):
    factor_of = 1.0
    for axis_at, blocks in cuts:
        draws = jax.random.uniform(jax.random.fold_in(jax.random.fold_in(stream_key, 6), axis_at), (blocks,), jnp.float32, low / len(cuts), high / len(cuts))
        factor_of = factor_of * jnp.repeat(jnp.exp(draws), dims[axis_at] // blocks).reshape((-1,) + (1,) * (len(dims) - 1 - axis_at))
    return factor_of


def routed_block(rng, own, number, rows, number_of, top, most, slope):
    order = jax.random.permutation(rng, number_of)
    heavy_load, usual = portions_of(number_of, rows * top, most, slope, True), portions_of(number_of, rows * top, most, slope, False)
    places = jnp.arange(number_of)

    def named(lengths, offset_by):
        used = int((lengths > 0).sum())
        fixed = max(1, used // 4)
        moved = fixed + (places - fixed + offset_by * (used - fixed)) % max(1, number_of - fixed)
        return jnp.zeros((number_of,), jnp.int32).at[order[jnp.where(places < fixed, places, moved)]].set(jnp.asarray(lengths, jnp.int32))

    lengths = jnp.where(number % 4 == 0, named(heavy_load, number // 4), named(usual, number - number // 4 - 1))
    mixed = jax.random.permutation(jax.random.fold_in(own, 3), number_of)
    source_of, taker = mixed[0:number_of // 2 * 2:2], mixed[1:number_of // 2 * 2:2]
    margin = jnp.minimum(lengths[source_of] - 1, most - lengths[taker]) // 2
    margin = jnp.where((source_of == order[0]) | (taker == order[0]) | (lengths[taker] == 0), 0, jnp.maximum(margin, 0))
    moved = jax.random.randint(jax.random.fold_in(own, 4), (number_of // 2,), 0, 1 << 20) % (margin + 1)
    lengths = lengths.at[source_of].add(-moved).at[taker].add(moved)
    members = jnp.searchsorted(jnp.cumsum(lengths), jnp.arange(rows * top), side="right").astype(jnp.int32)
    grid = members.reshape(top, rows).T
    grid = grid[jax.random.permutation(jax.random.fold_in(own, 1), rows)]
    offset_by = jax.random.randint(jax.random.fold_in(own, 2), (rows, 1), 0, top)
    return jnp.take_along_axis(grid, (jnp.arange(top)[None, :] + offset_by) % top, axis=1)


def portions_of(number_of, total, limit, skew, full):
    weights = [(1 << 20) // math.isqrt(standing ** skew) + 1 for standing in range(1, number_of + 1)]
    largest = limit if full else min(limit, max(-(-total // number_of), total * weights[0] // sum(weights)))
    least = 1 if total - largest >= number_of - 1 else 0
    holding, spare = [largest] + [least] * (number_of - 1), total - largest - least * (number_of - 1)
    while spare > 0:
        candidates = [i for i in range(1, number_of) if holding[i] < largest] or [i for i in range(1, number_of) if holding[i] < limit]
        mass, remaining = sum([weights[i] for i in candidates]), spare
        for i in candidates:
            addition = min(limit - holding[i], max(1, remaining * weights[i] // mass), spare)
            holding[i] = holding[i] + addition
            spare = spare - addition
    return np.array(holding)


def centred(rng, extent, deviation, limit, cuts=(), kind=jnp.bfloat16):
    drawn = deviation * jax.random.normal(rng, extent, jnp.float32)
    if cuts:
        drawn = drawn * block_levels(rng, extent, cuts, -0.22, 0.18)
    return jnp.clip(drawn, -limit, limit).astype(kind)


def setup_inputs(seed: int = 0) -> dict:
    arg_keys = jax.random.split(jax.random.key(seed), 10)
    velocity = centred(arg_keys[0], (3, 512, ELEMS), 0.2, 1.1953125, ((2, 32),))
    inverse_sizes = jnp.clip(jnp.exp(math.log(2.0) - 1.3862944 * jax.random.uniform(arg_keys[1], (3, ELEMS), jnp.float32) ** block_levels(arg_keys[1], (3, ELEMS), ((1, 32),), -0.2, 0.2)), 0.5, 2.0)
    resample_x = jnp.clip(0.25 * jax.random.uniform(arg_keys[2], (2, 8, 8, ELEMS), jnp.float32) ** block_levels(arg_keys[2], (2, 8, 8, ELEMS), ((3, 32),), -0.2, 0.2), 0.0, 0.25)
    resample_y = jnp.clip(0.25 * jax.random.uniform(arg_keys[3], (2, 4, 8, ELEMS), jnp.float32) ** block_levels(arg_keys[3], (2, 4, 8, ELEMS), ((3, 32),), -0.2, 0.2), 0.0, 0.25)
    resample_z = jnp.clip(0.25 * jax.random.uniform(arg_keys[4], (2, 4, 8, ELEMS), jnp.float32) ** block_levels(arg_keys[4], (2, 4, 8, ELEMS), ((3, 32),), -0.2, 0.2), 0.0, 0.25)
    piece_target = draw_piece_target(jax.random.fold_in(arg_keys[9], 71), 0)
    target_brick_keys = jax.random.split(jax.random.fold_in(arg_keys[6], 1), ELEMS // E_DEV)
    target_brick_turns = jax.random.permutation(jax.random.fold_in(arg_keys[6], 3), ELEMS // E_DEV)
    target_brick = jax.vmap(lambda own, number: routed_block(jax.random.fold_in(arg_keys[6], 2), own, number, E_DEV, NBRICKS, 1, CAPT, 2))(target_brick_keys, target_brick_turns).reshape((ELEMS, 1))
    target_block = with_ends(jax.random.randint(arg_keys[7], (ELEMS,), 0, BLOCKS), jax.random.fold_in(arg_keys[7], 1), 0, BLOCKS - 1).astype(jnp.int32)
    brick_home = jax.random.permutation(arg_keys[8], NBRICKS).astype(jnp.int32)
    return dict(velocity=velocity, inverse_sizes=inverse_sizes, resample_x=resample_x, resample_y=resample_y, resample_z=resample_z, piece_target=piece_target, target_brick=target_brick, target_block=target_block, brick_home=brick_home)


GLL_NODES = [-1.0, -0.8717401485096066, -0.5917001814331423, -0.2092992179024789, 0.2092992179024789, 0.5917001814331423, 0.8717401485096066, 1.0]

def derivative_operator():
    barycentric = []
    for first in range(8):
        product_term = 1.0
        for other in range(8):
            if other != first:
                product_term = product_term * (GLL_NODES[first] - GLL_NODES[other])
        barycentric.append(1.0 / product_term)
    matrix_rows = []
    for first in range(8):
        row_values = []
        for second in range(8):
            if second == first:
                row_values.append(0.0)
            else:
                row_values.append(barycentric[second] / barycentric[first] / (GLL_NODES[first] - GLL_NODES[second]))
        row_values[first] = -sum(row_values)
        matrix_rows.append(row_values)
    diff_matrix = np.array(matrix_rows)
    identity = np.eye(8)
    return np.concatenate([np.kron(np.kron(diff_matrix, identity), identity), np.kron(np.kron(identity, diff_matrix), identity), np.kron(np.kron(identity, identity), diff_matrix)], axis=0)

def stitch_stream(gradient, from_prev, from_next):
    low_face = gradient[:, 0]
    high_face = gradient[:, 7]
    from_below = jnp.concatenate([from_prev[:, :, None, :], high_face[:, :, :-1, :]], axis=2)
    from_above = jnp.concatenate([low_face[:, :, 1:, :], from_next[:, :, None, :]], axis=2)
    return gradient.at[:, 0].set(low_face + from_below).at[:, 7].set(high_face + from_above)

def middle_eigen(gradient):
    strain = [[0.5 * (gradient[first][second] + gradient[second][first]) for second in range(3)] for first in range(3)]
    rotation = [[0.5 * (gradient[first][second] - gradient[second][first]) for second in range(3)] for first in range(3)]
    moment = [[sum((strain[first][inner] * strain[inner][second] + rotation[first][inner] * rotation[inner][second] for inner in range(3))) for second in range(3)] for first in range(3)]
    mean_diag = (moment[0][0] + moment[1][1] + moment[2][2]) / 3.0
    shift_x = moment[0][0] - mean_diag
    shift_y = moment[1][1] - mean_diag
    shift_z = moment[2][2] - mean_diag
    offdiag = moment[0][1] * moment[0][1] + moment[0][2] * moment[0][2] + moment[1][2] * moment[1][2]
    spread = (shift_x * shift_x + shift_y * shift_y + shift_z * shift_z + 2.0 * offdiag) / 6.0
    determinant = shift_x * (shift_y * shift_z - moment[1][2] * moment[1][2]) - moment[0][1] * (moment[0][1] * shift_z - moment[1][2] * moment[0][2]) + moment[0][2] * (moment[0][1] * moment[1][2] - shift_y * moment[0][2])
    halfdet = 0.5 * determinant
    discrim = jnp.maximum(spread * spread * spread - halfdet * halfdet, 0.0)
    angles = jnp.arctan2(jnp.sqrt(discrim), halfdet) / 3.0
    radius = 2.0 * jnp.sqrt(spread)
    largest = mean_diag + radius * jnp.cos(angles)
    smallest = mean_diag + radius * jnp.cos(angles + 2.0 * math.pi / 3.0)
    return 3.0 * mean_diag - largest - smallest

def resample(lambda_two, weight_x, weight_y, weight_z):
    highest = lax.Precision.HIGHEST
    along_x = jnp.einsum('oaie,ijke->oajke', weight_x, lambda_two, precision=highest)
    along_y = jnp.einsum('obje,oajke->oabke', weight_y, along_x, precision=highest)
    along_z = jnp.einsum('ocke,oabke->oabce', weight_z, along_y, precision=highest)
    columns = lambda_two.shape[-1]
    return jnp.transpose(along_z.reshape(2, 128, columns), (0, 2, 1))

def slab_gradients(operator, slab_velocity, slab_sizes):
    products = jnp.einsum('pq,cqe->cpe', operator.astype(jnp.float32), slab_velocity.astype(jnp.float32), precision=lax.Precision.HIGHEST)
    columns = slab_velocity.shape[2]
    scaled = products.reshape(3, 3, 512, columns) * slab_sizes[None, :, None, :]
    return scaled.reshape(9, 8, 64, LAYERS, CROSS)

def stitch_cross_grid(gradient):
    shaped = gradient.reshape(9, 8, 8, 8, LAYERS, EYN, EZN)
    low_face = shaped[:, :, 0]
    high_face = shaped[:, :, 7]
    zero_row = jnp.zeros_like(high_face[..., :1, :])
    from_below = jnp.concatenate([zero_row, high_face[..., :-1, :]], axis=-2)
    from_above = jnp.concatenate([low_face[..., 1:, :], zero_row], axis=-2)
    shaped = shaped.at[:, :, 0].set(low_face + from_below).at[:, :, 7].set(high_face + from_above)
    low_face = shaped[:, :, :, 0]
    high_face = shaped[:, :, :, 7]
    shaped = shaped.at[:, :, :, 0].set(low_face + jnp.roll(high_face, 1, axis=-1)).at[:, :, :, 7].set(high_face + jnp.roll(low_face, -1, axis=-1))
    points = jnp.arange(8, dtype=jnp.int32)
    on_face = (points == 0) | (points == 7)
    normal = jnp.arange(EYN, dtype=jnp.int32)
    at_wall = (points[:, None] == 0) & (normal[None, :] == 0) | (points[:, None] == 7) & (normal[None, :] == EYN - 1)
    mult_x = jnp.where(on_face, 2.0, 1.0)
    mult_y = jnp.where(on_face[:, None] & jnp.logical_not(at_wall), 2.0, 1.0)
    shaped = shaped / mult_x[None, :, None, None, None, None, None]
    shaped = shaped / mult_y[None, None, :, None, None, :, None]
    shaped = shaped / mult_x[None, None, None, :, None, None, None]
    return shaped

def reference(velocity, inverse_sizes, resample_x, resample_y, resample_z, piece_target, target_brick, target_block, brick_home):
    operator = jnp.asarray(derivative_operator(), jnp.float32).astype(jnp.bfloat16)
    per_dev = LAYERS * CROSS
    slabs = velocity.shape[2] // per_dev

    def by_slab(values):
        leading = values.shape[:-1]
        return jnp.moveaxis(values.reshape(leading + (slabs, per_dev)), -2, 0)
    vel_slabs = by_slab(velocity)
    size_slabs = by_slab(inverse_sizes)

    def rim_pass(inputs):
        gradient = slab_gradients(operator, inputs[0], inputs[1])
        return jnp.stack([gradient[:, 0, :, 0, :], gradient[:, 7, :, LAYERS - 1, :]], axis=2)
    rim_faces = lax.map(rim_pass, (vel_slabs, size_slabs))
    from_prev = jnp.roll(rim_faces[:, :, :, 1, :], 1, axis=0)
    from_next = jnp.roll(rim_faces[:, :, :, 0, :], -1, axis=0)

    def piece_pass(inputs):
        slab_vel, slab_size, weight_x, weight_y, weight_z, prev_face, next_face = inputs
        gradient = slab_gradients(operator, slab_vel, slab_size)
        gradient = stitch_stream(gradient, prev_face, next_face)
        gradient = stitch_cross_grid(gradient)
        lambda_two = middle_eigen(gradient.reshape(3, 3, 512, per_dev))
        return resample(lambda_two.reshape(8, 8, 8, per_dev), weight_x, weight_y, weight_z)
    pieces = lax.map(piece_pass, (vel_slabs, size_slabs, by_slab(resample_x), by_slab(resample_y), by_slab(resample_z), from_prev, from_next))
    local_ids = jnp.moveaxis(piece_target.reshape(2, slabs, per_dev), 1, 0)
    offsets = (jnp.arange(slabs, dtype=jnp.int32) * per_dev)[:, None, None]
    targets = (local_ids + offsets).reshape(-1).astype(jnp.int32)
    home_rows = brick_home[target_brick[targets, 0]]
    blocks = target_block[targets]
    bricks = jnp.zeros((NBRICKS, BLOCKS, 128), jnp.float32)
    return bricks.at[home_rows, blocks].add(pieces.reshape(-1, 128))
```

```python
import functools
import math

import jax
import jax.numpy as jnp
import ml_dtypes
import numpy as np
from jax import lax
from jax.experimental import pallas as pl
from jax.experimental.pallas import tpu as pltpu
from jax.sharding import PartitionSpec as P

EYN = 8
EZN = 16
CROSS = EYN * EZN
BLOCKS = 2048
F32 = jnp.float32
BF16 = jnp.bfloat16

GLL_NODES = [
    -1.0,
    -0.8717401485096066,
    -0.5917001814331423,
    -0.2092992179024789,
    0.2092992179024789,
    0.5917001814331423,
    0.8717401485096066,
    1.0,
]

ORDER = [0, 1, 2, 3, 7, 4, 5, 6]


def derivative_operator():
    barycentric = []
    for first in range(8):
        product_term = 1.0
        for other in range(8):
            if other != first:
                product_term = product_term * (GLL_NODES[first] - GLL_NODES[other])
        barycentric.append(1.0 / product_term)
    matrix_rows = []
    for first in range(8):
        row_values = []
        for second in range(8):
            if second == first:
                row_values.append(0.0)
            else:
                row_values.append(
                    barycentric[second]
                    / barycentric[first]
                    / (GLL_NODES[first] - GLL_NODES[second])
                )
        row_values[first] = -sum(row_values)
        matrix_rows.append(row_values)
    diff_matrix = np.array(matrix_rows)
    identity = np.eye(8)
    return np.concatenate(
        [
            np.kron(np.kron(diff_matrix, identity), identity),
            np.kron(np.kron(identity, diff_matrix), identity),
            np.kron(np.kron(identity, identity), diff_matrix),
        ],
        axis=0,
    )


def operators():
    rounded = derivative_operator().astype(np.float32).astype(ml_dtypes.bfloat16).astype(np.float32)
    ends = np.ones(8, np.float32)
    ends[0] = ends[7] = 0.5
    halves = ends[:, None, None] * ends[None, :, None] * ends[None, None, :]
    rows = rounded.reshape(3, 8, 8, 8, 512) * halves[None, :, :, :, None]
    rows = rows.transpose(0, 2, 3, 1, 4)[:, :, ORDER]
    whole = rows[:, :, :, ORDER].reshape(3, 512, 512)
    faces = np.stack([rows[:, :, :, 0], rows[:, :, :, 7]]).reshape(384, 512)
    return whole.astype(ml_dtypes.bfloat16), faces.astype(ml_dtypes.bfloat16)


def third_angle():
    spots = (1.0 - np.cos(np.pi * (np.arange(4000) + 0.5) / 4000)) / 2
    values = np.sin(np.arcsin(1.0 - spots * spots) / 3.0)
    fitted = np.polynomial.chebyshev.Chebyshev.fit(spots, values, 9, domain=[0, 1])
    return [float(c) for c in fitted.convert(kind=np.polynomial.Polynomial).coef]


THIRD = third_angle()


def dot(left, right):
    return lax.dot_general(left, right, (((1,), (0,)), ((), ())), preferred_element_type=F32)


def dot_nt(left, right):
    return lax.dot_general(left, right, (((1,), (1,)), ((), ())), preferred_element_type=F32)


def iota(shape, axis):
    return lax.broadcasted_iota(jnp.int32, shape, axis)


def onehot(mask):
    return jnp.where(mask, 1.0, 0.0).astype(BF16)


def halves_of(values):
    high = values.astype(BF16)
    return high, (values - high.astype(F32)).astype(BF16)


def normal_sums(low, high):
    normal = iota(low.shape, 1) // EZN
    below = pltpu.roll(high, EZN, 1)
    above = pltpu.roll(low, CROSS - EZN, 1)
    return (
        low + jnp.where(normal == 0, low, below),
        high + jnp.where(normal == EYN - 1, high, above),
    )


def from_before(values):
    spanwise = iota(values.shape, 1) % EZN
    return jnp.where(
        spanwise == 0, pltpu.roll(values, CROSS + 1 - EZN, 1), pltpu.roll(values, 1, 1)
    )


def from_after(values):
    spanwise = iota(values.shape, 1) % EZN
    return jnp.where(
        spanwise == EZN - 1, pltpu.roll(values, EZN - 1, 1), pltpu.roll(values, CROSS - 1, 1)
    )


def rim_kernel(faces_ref, first_ref, last_ref, sizes_first, sizes_last, lo_first, hi_first, lo_last, hi_last):
    sub = iota((64, CROSS), 0) % 8
    for vel, sizes, outs in (
        (first_ref, sizes_first, (lo_first, hi_first)),
        (last_ref, sizes_last, (lo_last, hi_last)),
    ):
        for c in range(3):
            products = dot(faces_ref[...], vel[c])
            for face in range(2):
                for a in range(3):
                    at = (face * 3 + a) * 64
                    part = products[at : at + 64] * sizes[a : a + 1, :]
                    low, high = normal_sums(part[:8], part[56:])
                    part = jnp.concatenate([low, part[8:56], high], axis=0)
                    swapped = jnp.where(sub == 0, from_after(part), from_before(part))
                    swapped = pltpu.roll(swapped.reshape(8, 8, CROSS), 4, 1).reshape(64, CROSS)
                    part = part + jnp.where((sub == 0) | (sub == 4), swapped, 0.0)
                    outs[face][pl.ds((c * 3 + a) * 64, 64), :] = part


def route_kernel(capacity, pt_ref, brick_ref, block_ref, home_ref, slot_ref, ids_ref):
    targets = brick_ref.shape[1]
    bricks = home_ref.shape[0]
    devices = ids_ref.shape[0]
    named = iota((bricks, targets), 0) == brick_ref[...]
    named_f = jnp.where(named, 1.0, 0.0)
    earlier = onehot(iota((targets, targets), 0) < iota((targets, targets), 1))
    ranks = dot(named_f.astype(BF16), earlier)
    owner = jnp.sum(named_f * home_ref[...].astype(F32), axis=0, keepdims=True)
    rank = jnp.sum(named_f * ranks, axis=0, keepdims=True)
    row = iota((8, targets), 0)
    both = jnp.where(row == 0, owner, jnp.where(row == 1, rank, 0.0)).astype(BF16)
    for o in range(2):
        picked = onehot(iota((targets, targets), 0) == pt_ref[o : o + 1, :])
        found = dot(both, picked)
        slot_ref[o : o + 1, :] = (found[0:1] * capacity + found[1:2]).astype(jnp.int32)
    owned = jnp.where(iota((devices, targets), 0) == owner.astype(jnp.int32), 1.0, 0.0)
    placed = onehot(iota((capacity, targets), 0) == rank.astype(jnp.int32))
    block = block_ref[...]
    upper = (block // 64).astype(F32)
    lower = (block % 64).astype(F32)
    ids = (
        dot_nt((owned * upper).astype(BF16), placed) * 64.0
        + dot_nt((owned * lower).astype(BF16), placed)
        + dot_nt(owned.astype(BF16), placed)
        - 1.0
    )
    ids_ref[...] = ids.astype(jnp.int32)


def middle_eigen(g):
    s01, s02, s12 = g[0][1] + g[1][0], g[0][2] + g[2][0], g[1][2] + g[2][1]
    p01, p02, p12 = g[0][1] * g[1][0], g[0][2] * g[2][0], g[1][2] * g[2][1]
    m00 = g[0][0] * g[0][0] + (p01 + p02)
    m11 = g[1][1] * g[1][1] + (p01 + p12)
    m22 = g[2][2] * g[2][2] + (p02 + p12)
    m01 = 0.5 * ((g[0][0] + g[1][1]) * s01 + g[0][2] * g[2][1] + g[1][2] * g[2][0])
    m02 = 0.5 * ((g[0][0] + g[2][2]) * s02 + g[0][1] * g[1][2] + g[2][1] * g[1][0])
    m12 = 0.5 * ((g[1][1] + g[2][2]) * s12 + g[1][0] * g[0][2] + g[2][0] * g[0][1])
    q = (m00 + m11 + m22) * (1.0 / 3.0)
    x, y, z = m00 - q, m11 - q, m22 - q
    n01, n02, n12 = m01 * m01, m02 * m02, m12 * m12
    spread = (x * x + y * y + z * z + 2.0 * (n01 + n02 + n12)) * (1.0 / 6.0)
    halfdet = 0.5 * (x * (y * z - n12) - z * n01 - y * n02) + m01 * m02 * m12
    inverse = lax.rsqrt(jnp.maximum(spread, 1e-37))
    ratio = jnp.abs(halfdet) * inverse * inverse * inverse
    gap = jnp.maximum(1.0 - ratio, 1e-30)
    root = gap * lax.rsqrt(gap)
    third = THIRD[-1]
    for coefficient in THIRD[-2::-1]:
        third = third * root + coefficient
    turn = 2.0 * (spread * inverse) * third
    return jnp.where(halfdet < 0.0, q + turn, q - turn)


def slab_pieces(count, op_ref, vels, sizes, rxs, rys, rzs, belows, aboves, part, lam, along, store):
    joined = [
        jnp.concatenate([vels[l][c] for l in range(count)], axis=1) if count > 1 else vels[0][c]
        for c in range(3)
    ]
    for c in range(3):
        for a in range(3):
            products = dot(op_ref[a], joined[c])
            for l in range(count):
                part[l, pl.ds((c * 3 + a) * 512, 512), :] = (
                    products[:, l * CROSS : (l + 1) * CROSS] * sizes[l][a : a + 1, :]
                )

    def stitch(ca, l):
        at = ca * 512
        low, high = normal_sums(part[l, pl.ds(at, 64), :], part[l, pl.ds(at + 448, 64), :])
        part[l, pl.ds(at, 64), :] = low
        part[l, pl.ds(at + 448, 64), :] = high
        for j in range(8):
            near, far = pl.ds(at + j * 64, 8), pl.ds(at + j * 64 + 32, 8)
            low, high = part[l, near, :], part[l, far, :]
            part[l, near, :] = low + from_before(high)
            part[l, far, :] = high + from_after(low)

    for l in range(count):
        lax.fori_loop(0, 9, lambda ca, carry, l=l: (stitch(ca, l), carry)[1], 0)

    def face_row(source, which, l, ca, jk):
        if source is not None:
            return source[pl.ds(ca * 64 + jk, 1), :]
        return part[l, pl.ds(ca * 512 + jk * 8 + which, 1), :]

    sub = iota((8, CROSS), 0)

    def point_row(jk, l):
        g = []
        for ca in range(9):
            below = face_row(belows[l], 4, l - 1, ca, jk)
            above = face_row(aboves[l], 0, l + 1, ca, jk)
            g.append(
                part[l, pl.ds(ca * 512 + jk * 8, 8), :]
                + jnp.where(sub == 0, below, jnp.where(sub == 4, above, 0.0))
            )
        lam[pl.ds(jk * 8, 8), :] = middle_eigen([g[0:3], g[3:6], g[6:9]])

    for l in range(count):
        lax.fori_loop(0, 64, lambda jk, carry, l=l: (point_row(jk, l), carry)[1], 0, unroll=2)
        for o in range(2):
            for j in range(8):
                rows = [lam[pl.ds((j * 8 + k) * 8, 8), :] for k in range(8)]
                for w in range(4):
                    total = rows[0] * rzs[l][o, w, ORDER[0] : ORDER[0] + 1, :]
                    for k in range(1, 8):
                        total = total + rows[k] * rzs[l][o, w, ORDER[k] : ORDER[k] + 1, :]
                    along[0, pl.ds((w * 8 + j) * 8, 8), :] = total
            for w in range(4):
                rows = [along[0, pl.ds((w * 8 + j) * 8, 8), :] for j in range(8)]
                for v in range(4):
                    total = rows[0] * rys[l][o, v, 0:1, :]
                    for j in range(1, 8):
                        total = total + rows[j] * rys[l][o, v, j : j + 1, :]
                    along[1, pl.ds((v * 4 + w) * 8, 8), :] = total
            rows = [along[1, pl.ds(i, 16, stride=8), :] for i in range(8)]
            for u in range(8):
                total = rows[0] * rxs[l][o, u, ORDER[0] : ORDER[0] + 1, :]
                for i in range(1, 8):
                    total = total + rows[i] * rxs[l][o, u, ORDER[i] : ORDER[i] + 1, :]
                high, low = halves_of(total)
                columns = pl.ds((l * 2 + o) * CROSS, CROSS)
                store[pl.ds(u * 16, 16), columns] = high
                store[pl.ds(128 + u * 16, 16), columns] = low


def split_refs(refs, count):
    groups = []
    for _ in range(5):
        groups.append(refs[:count])
        refs = refs[count:]
    return groups, refs


def inner_kernel(count, *refs):
    op_ref, refs = refs[0], refs[1:]
    (vels, sizes, rxs, rys, rzs), refs = split_refs(refs, count)
    below, above, store, lo_out, hi_out, part, lam, along = refs
    belows = [below] + [None] * (count - 1)
    aboves = [None] * (count - 1) + [above]
    slab_pieces(count, op_ref, vels, sizes, rxs, rys, rzs, belows, aboves, part, lam, along, store)
    lo_out[...] = part[0, pl.ds(0, 576, stride=8), :]
    hi_out[...] = part[count - 1, pl.ds(4, 576, stride=8), :]


def outer_kernel(layers, *refs):
    op_ref, refs = refs[0], refs[1:]
    (vels, sizes, rxs, rys, rzs), refs = split_refs(refs, 2)
    below_first, above_first, below_last, above_last, slots, inner, send, part, lam, along, store = refs
    slab_pieces(
        2, op_ref, vels, sizes, rxs, rys, rzs, [below_first, below_last], [above_first, above_last], part, lam, along, store
    )
    rows = iota((send.shape[0], CROSS), 0)

    def chosen(which):
        return jnp.concatenate(
            [
                onehot(rows == slots[o : o + 1, l * CROSS : (l + 1) * CROSS])
                for l in which
                for o in range(2)
            ],
            axis=1,
        )

    both = dot_nt(chosen(range(1, layers - 1)), inner[...]) + dot_nt(chosen((0, layers - 1)), store[...])
    send[...] = both[:, :128] + both[:, 128:]


def gather_kernel(ids_ref, rows_ref, out_ref, halves):
    high, low = halves_of(rows_ref[...])
    halves[:, :128] = high
    halves[:, 128:] = low
    step = 256

    def chunk(i, carry):
        named = onehot(iota((step, ids_ref.shape[1]), 0) + i * step == ids_ref[...])
        both = dot(named, halves[...])
        out_ref[pl.ds(pl.multiple_of(i * step, step), step), :] = both[:, :128] + both[:, 128:]
        return carry

    lax.fori_loop(0, BLOCKS // step, chunk, 0)


def params():
    return pltpu.CompilerParams(vmem_limit_bytes=48 * 1024 * 1024)


def whole_spec(shape):
    return pl.BlockSpec(shape, lambda i: (0,) * len(shape))


def layer_spec(array, layer):
    lead = array.shape[:-1]
    return pl.BlockSpec(lead + (CROSS,), lambda i: (0,) * len(lead) + (layer,))


def shards(
    velocity,
    inverse_sizes,
    resample_x,
    resample_y,
    resample_z,
    piece_target,
    target_brick,
    target_block,
    brick_home,
):
    elements = velocity.shape[2]
    layers = elements // CROSS
    devices = lax.axis_size("dom")
    capacity = max(2, 4 * elements // devices)
    whole, faces = (jnp.asarray(o) for o in operators())
    face_shape = jax.ShapeDtypeStruct((576, CROSS), F32)
    last = layers - 1

    lo_first, hi_first, lo_last, hi_last = pl.pallas_call(
        rim_kernel,
        grid=(1,),
        in_specs=[
            whole_spec(faces.shape),
            layer_spec(velocity, 0),
            layer_spec(velocity, last),
            layer_spec(inverse_sizes, 0),
            layer_spec(inverse_sizes, last),
        ],
        out_specs=[whole_spec((576, CROSS))] * 4,
        out_shape=[face_shape] * 4,
        compiler_params=params(),
        name="rim_faces",
    )(faces, velocity, velocity, inverse_sizes, inverse_sizes)
    from_prev = lax.ppermute(hi_last, "dom", [(i, (i + 1) % devices) for i in range(devices)])
    from_next = lax.ppermute(lo_first, "dom", [((i + 1) % devices, i) for i in range(devices)])

    slots, ids = pl.pallas_call(
        functools.partial(route_kernel, capacity),
        out_shape=[
            jax.ShapeDtypeStruct((2, elements), jnp.int32),
            jax.ShapeDtypeStruct((devices, capacity), jnp.int32),
        ],
        compiler_params=params(),
        name="routes",
    )(
        piece_target,
        target_brick.reshape(1, elements),
        target_block.reshape(1, elements),
        brick_home.reshape(-1, 1),
    )
    received_ids = lax.all_to_all(ids, "dom", split_axis=0, concat_axis=0, tiled=True)

    arrays = (velocity, inverse_sizes, resample_x, resample_y, resample_z)

    def scratch(count):
        return [
            pltpu.VMEM((count, 4608, CROSS), F32),
            pltpu.VMEM((512, CROSS), F32),
            pltpu.VMEM((2, 256, CROSS), F32),
        ]

    def layer_operands(which):
        specs = [layer_spec(array, l) for array in arrays for l in which]
        return specs, [array for array in arrays for _ in which]

    inside = range(1, last)
    specs, operands = layer_operands(inside)
    inner, lo_inner, hi_inner = pl.pallas_call(
        functools.partial(inner_kernel, len(inside)),
        grid=(1,),
        in_specs=[whole_spec(whole.shape)] + specs + [whole_spec((576, CROSS))] * 2,
        out_specs=[whole_spec((256, len(inside) * 256)), whole_spec((576, CROSS)), whole_spec((576, CROSS))],
        out_shape=[jax.ShapeDtypeStruct((256, len(inside) * 256), BF16), face_shape, face_shape],
        scratch_shapes=scratch(len(inside)),
        compiler_params=params(),
        name="inner_layers",
    )(whole, *operands, hi_first, lo_last)

    specs, operands = layer_operands((0, last))
    rows = devices * capacity
    sendbuf = pl.pallas_call(
        functools.partial(outer_kernel, layers),
        grid=(1,),
        in_specs=[whole_spec(whole.shape)]
        + specs
        + [whole_spec((576, CROSS))] * 4
        + [whole_spec(slots.shape), whole_spec(inner.shape)],
        out_specs=whole_spec((rows, 128)),
        out_shape=jax.ShapeDtypeStruct((rows, 128), F32),
        scratch_shapes=scratch(2) + [pltpu.VMEM((256, 512), BF16)],
        compiler_params=params(),
        name="outer_layers",
    )(whole, *operands, from_prev, lo_inner, hi_inner, from_next, slots, inner)

    received = lax.all_to_all(
        sendbuf.reshape(devices, capacity, 128), "dom", split_axis=0, concat_axis=0, tiled=True
    )
    image = pl.pallas_call(
        gather_kernel,
        out_shape=jax.ShapeDtypeStruct((BLOCKS, 128), F32),
        scratch_shapes=[pltpu.VMEM((rows, 256), BF16)],
        compiler_params=params(),
        name="block_sums",
    )(received_ids.reshape(1, rows), received.reshape(rows, 128))
    return image[None]


def solution(mesh):
    return jax.shard_map(
        shards,
        mesh=mesh,
        in_specs=(
            P(None, None, "dom"),
            P(None, "dom"),
            P(None, None, None, "dom"),
            P(None, None, None, "dom"),
            P(None, None, None, "dom"),
            P(None, "dom"),
            P("dom", None),
            P("dom"),
            P(),
        ),
        out_specs=P("dom", None, None),
        check_vma=False,
    )
```

```python
import functools
import math

import jax
import jax.numpy as jnp
import ml_dtypes
import numpy as np
from jax import lax
from jax.experimental import pallas as pl
from jax.experimental.pallas import tpu as pltpu
from jax.sharding import PartitionSpec as P

EYN = 8
EZN = 16
CROSS = EYN * EZN
BLOCKS = 2048
F32 = jnp.float32
BF16 = jnp.bfloat16

GLL_NODES = [
    -1.0,
    -0.8717401485096066,
    -0.5917001814331423,
    -0.2092992179024789,
    0.2092992179024789,
    0.5917001814331423,
    0.8717401485096066,
    1.0,
]

ORDER = [0, 1, 2, 3, 7, 4, 5, 6]


def derivative_operator():
    barycentric = []
    for first in range(8):
        product_term = 1.0
        for other in range(8):
            if other != first:
                product_term = product_term * (GLL_NODES[first] - GLL_NODES[other])
        barycentric.append(1.0 / product_term)
    matrix_rows = []
    for first in range(8):
        row_values = []
        for second in range(8):
            if second == first:
                row_values.append(0.0)
            else:
                row_values.append(
                    barycentric[second]
                    / barycentric[first]
                    / (GLL_NODES[first] - GLL_NODES[second])
                )
        row_values[first] = -sum(row_values)
        matrix_rows.append(row_values)
    diff_matrix = np.array(matrix_rows)
    identity = np.eye(8)
    return np.concatenate(
        [
            np.kron(np.kron(diff_matrix, identity), identity),
            np.kron(np.kron(identity, diff_matrix), identity),
            np.kron(np.kron(identity, identity), diff_matrix),
        ],
        axis=0,
    )


def operators():
    rounded = derivative_operator().astype(np.float32).astype(ml_dtypes.bfloat16).astype(np.float32)
    ends = np.ones(8, np.float32)
    ends[0] = ends[7] = 0.5
    halves = ends[:, None, None] * ends[None, :, None] * ends[None, None, :]
    rows = rounded.reshape(3, 8, 8, 8, 512) * halves[None, :, :, :, None]
    rows = rows.transpose(0, 2, 3, 1, 4)[:, :, ORDER]
    whole = rows[:, :, :, ORDER].reshape(3, 512, 512)
    faces = np.stack([rows[:, :, :, 0], rows[:, :, :, 7]]).reshape(384, 512)
    return whole.astype(ml_dtypes.bfloat16), faces.astype(ml_dtypes.bfloat16)


def third_angle():
    spots = (1.0 - np.cos(np.pi * (np.arange(4000) + 0.5) / 4000)) / 2
    values = np.sin(np.arcsin(1.0 - spots * spots) / 3.0)
    fitted = np.polynomial.chebyshev.Chebyshev.fit(spots, values, 9, domain=[0, 1])
    return [float(c) for c in fitted.convert(kind=np.polynomial.Polynomial).coef]


THIRD = third_angle()


def dot(left, right):
    return lax.dot_general(left, right, (((1,), (0,)), ((), ())), preferred_element_type=F32)


def dot_nt(left, right):
    return lax.dot_general(left, right, (((1,), (1,)), ((), ())), preferred_element_type=F32)


def iota(shape, axis):
    return lax.broadcasted_iota(jnp.int32, shape, axis)


def onehot(mask):
    return jnp.where(mask, 1.0, 0.0).astype(BF16)


def halves_of(values):
    high = values.astype(BF16)
    return high, (values - high.astype(F32)).astype(BF16)


def normal_sums(low, high):
    normal = iota(low.shape, 1) // EZN
    below = pltpu.roll(high, EZN, 1)
    above = pltpu.roll(low, CROSS - EZN, 1)
    return (
        low + jnp.where(normal == 0, low, below),
        high + jnp.where(normal == EYN - 1, high, above),
    )


def span_lanes(step):
    lane = iota((8, CROSS), 1)
    return lane // EZN * EZN + (lane + step) % EZN


def moved(values, lanes):
    index = jnp.broadcast_to(lanes[None], (values.shape[0] // 8, 8, CROSS)).reshape(values.shape)
    return jnp.take_along_axis(values, index, axis=1, mode="promise_in_bounds")


def rim_kernel(last, faces_hbm, vel_hbm, sizes_hbm, lo_first, hi_first, lo_last, hi_last, faces, vel, sizes, made, sems):
    tiles = ((last, (lo_last, hi_last)), (0, (lo_first, hi_first)))
    copies = []

    def begin(source, target):
        copy = pltpu.make_async_copy(source, target, sems.at[len(copies)])
        copy.start()
        copies.append(copy)
        return copy

    waits = [begin(faces_hbm, faces)]
    for n, (l, _) in enumerate(tiles):
        columns = pl.ds(l * CROSS, CROSS)
        waits.append(begin(vel_hbm.at[:, :, columns], vel.at[n]))
        waits.append(begin(sizes_hbm.at[:, columns], sizes.at[n]))
    sub = iota((64, CROSS), 0) % 8
    before, after = span_lanes(EZN - 1), span_lanes(1)
    waits[0].wait()
    results = []
    for n, (l, outs) in enumerate(tiles):
        waits[1 + 2 * n].wait()
        waits[2 + 2 * n].wait()
        for c in range(3):
            products = dot(faces[...], vel[n, c])
            for face in range(2):
                for a in range(3):
                    at = (face * 3 + a) * 64
                    part = products[at : at + 64] * sizes[n, a : a + 1, :]
                    low, high = normal_sums(part[:8], part[56:])
                    part = jnp.concatenate([low, part[8:56], high], axis=0)
                    swapped = jnp.where(sub == 0, moved(part, after), moved(part, before))
                    swapped = pltpu.roll(swapped.reshape(8, 8, CROSS), 4, 1).reshape(64, CROSS)
                    part = part + jnp.where((sub == 0) | (sub == 4), swapped, 0.0)
                    made[n, face, pl.ds((c * 3 + a) * 64, 64), :] = part
        for face in range(2):
            results.append(begin(made.at[n, face], outs[face]))
    for copy in results:
        copy.wait()


def routes(devices, capacity, pt_ref, brick_ref, block_ref, home_ref):
    targets = brick_ref.shape[1]
    bricks = home_ref.shape[1]
    named = jnp.where(iota((bricks, targets), 0) == brick_ref[...], 1.0, 0.0)
    earlier = onehot(iota((targets, targets), 0) < iota((targets, targets), 1))
    ranks = dot(named.astype(BF16), earlier)
    homes = jnp.broadcast_to(home_ref[...].astype(F32), (8, bricks)).astype(BF16)
    owner = dot(homes, named.astype(BF16))[0:1]
    rank = jnp.sum(named * ranks, axis=0, keepdims=True)
    row = iota((8, targets), 0)
    both = jnp.where(row == 0, owner, jnp.where(row == 1, rank, 0.0)).astype(BF16)
    slots = []
    for o in range(2):
        picked = onehot(iota((targets, targets), 0) == pt_ref[o : o + 1, :])
        found = dot(both, picked)
        slots.append((found[0:1] * (capacity + 1) + found[1:2]).astype(jnp.int32))
    owned = jnp.where(iota((devices, targets), 0) == owner.astype(jnp.int32), 1.0, 0.0)
    placed = onehot(iota((128, targets), 0) == rank.astype(jnp.int32))
    block = block_ref[...]
    upper = (block // 64).astype(F32)
    lower = (block % 64).astype(F32)
    ids = (
        dot_nt((owned * upper).astype(BF16), placed) * 64.0
        + dot_nt((owned * lower).astype(BF16), placed)
        + dot_nt(owned.astype(BF16), placed)
        - 1.0
    )
    return slots, ids


def middle_eigen(g):
    s01, s02, s12 = g[0][1] + g[1][0], g[0][2] + g[2][0], g[1][2] + g[2][1]
    p01, p02, p12 = g[0][1] * g[1][0], g[0][2] * g[2][0], g[1][2] * g[2][1]
    m00 = g[0][0] * g[0][0] + (p01 + p02)
    m11 = g[1][1] * g[1][1] + (p01 + p12)
    m22 = g[2][2] * g[2][2] + (p02 + p12)
    m01 = 0.5 * ((g[0][0] + g[1][1]) * s01 + (g[0][2] * g[2][1] + g[1][2] * g[2][0]))
    m02 = 0.5 * ((g[0][0] + g[2][2]) * s02 + (g[0][1] * g[1][2] + g[2][1] * g[1][0]))
    m12 = 0.5 * ((g[1][1] + g[2][2]) * s12 + (g[1][0] * g[0][2] + g[2][0] * g[0][1]))
    q = (m00 + m11 + m22) * (1.0 / 3.0)
    x, y, z = m00 - q, m11 - q, m22 - q
    n01, n02, n12 = m01 * m01, m02 * m02, m12 * m12
    spread = (x * x + y * y + z * z + 2.0 * (n01 + n02 + n12)) * (1.0 / 6.0)
    halfdet = 0.5 * (x * (y * z - n12) - z * n01 - y * n02) + m01 * m02 * m12
    inverse = lax.rsqrt(jnp.maximum(spread, 1e-37))
    ratio = ((jnp.abs(halfdet) * inverse) * inverse) * inverse
    gap = jnp.maximum(1.0 - ratio, 1e-30)
    root = gap * lax.rsqrt(gap)
    pairs = [THIRD[n] + THIRD[n + 1] * root for n in range(0, 10, 2)]
    square = root * root
    fourth = square * square
    third = (pairs[0] + pairs[1] * square) + fourth * (
        (pairs[2] + pairs[3] * square) + fourth * pairs[4]
    )
    turn = 2.0 * (spread * inverse) * third
    return jnp.where(halfdet < 0.0, q + turn, q - turn)


def layer_pieces(layers, arrays, waits, belows, aboves, part, lam, along, store, before_stitch):
    op, vel, sizes, rx, ry, rz = arrays
    count = len(layers)
    lanes = [slice(l * CROSS, (l + 1) * CROSS) for l in layers]

    def joined(read):
        if layers[-1] - layers[0] == count - 1:
            return read(slice(lanes[0].start, lanes[-1].stop))
        return jnp.concatenate([read(at) for at in lanes], axis=1)

    before, after = span_lanes(EZN - 1), span_lanes(1)
    for c in range(3):
        velocities = joined(lambda at: vel[c, :, at])
        for a in range(3):
            products = dot(op[a], velocities) * joined(lambda at: sizes[a : a + 1, at])
            for l in range(count):
                values = products[:, l * CROSS : (l + 1) * CROSS]
                first, final = normal_sums(values[:64], values[448:])
                for j in range(8):
                    rows = {0: first, 7: final}.get(j, values[j * 64 : (j + 1) * 64])
                    near, far = rows[:8], rows[32:40]
                    at = (c * 3 + a) * 512 + j * 64
                    part[l, pl.ds(at, 8), :] = near + moved(far, before)
                    part[l, pl.ds(at + 8, 24), :] = rows[8:32]
                    part[l, pl.ds(at + 32, 8), :] = far + moved(near, after)
                    part[l, pl.ds(at + 40, 24), :] = rows[40:]
    before_stitch()
    for copy in waits:
        copy.wait()

    def face_sums(ca, carry):
        near, far = pl.ds(ca * 512, 64, stride=8), pl.ds(ca * 512 + 4, 64, stride=8)
        rows = pl.ds(ca * 64, 64)
        for l in range(count):
            if belows[l] is not None:
                part[l, near, :] = part[l, near, :] + belows[l][rows, :]
            if aboves[l] is not None:
                part[l, far, :] = part[l, far, :] + aboves[l][rows, :]
            else:
                shared = part[l, far, :] + part[l + 1, near, :]
                part[l, far, :] = shared
                part[l + 1, near, :] = shared
        return carry

    lax.fori_loop(0, 9, face_sums, 0, unroll=3)

    def point_row(jk, l):
        g = [part[l, pl.ds(ca * 512 + jk * 8, 8), :] for ca in range(9)]
        lam[pl.ds(jk * 8, 8), :] = middle_eigen([g[0:3], g[3:6], g[6:9]])

    for l in range(count):
        lax.fori_loop(0, 64, lambda jk, carry, l=l: (point_row(jk, l), carry)[1], 0, unroll=16)
        cols = lanes[l]
        for o in range(2):
            for j in range(8):
                rows = [lam[pl.ds((j * 8 + k) * 8, 8), :] for k in range(8)]
                for w in range(4):
                    total = rows[0] * rz[o, w, ORDER[0] : ORDER[0] + 1, cols]
                    for k in range(1, 8):
                        total = total + rows[k] * rz[o, w, ORDER[k] : ORDER[k] + 1, cols]
                    along[0, pl.ds((w * 8 + j) * 8, 8), :] = total
            for w in range(4):
                rows = [along[0, pl.ds((w * 8 + j) * 8, 8), :] for j in range(8)]
                for v in range(4):
                    total = rows[0] * ry[o, v, 0:1, cols]
                    for j in range(1, 8):
                        total = total + rows[j] * ry[o, v, j : j + 1, cols]
                    along[1, pl.ds((v * 4 + w) * 8, 8), :] = total
            rows = [along[1, pl.ds(i, 16, stride=8), :] for i in range(8)]
            for u in range(8):
                total = rows[0] * rx[o, u, ORDER[0] : ORDER[0] + 1, cols]
                for i in range(1, 8):
                    total = total + rows[i] * rx[o, u, ORDER[i] : ORDER[i] + 1, cols]
                high, low = halves_of(total)
                columns = pl.ds((l * 2 + o) * CROSS, CROSS)
                store[pl.ds(u * 16, 16), columns] = high
                store[pl.ds(128 + u * 16, 16), columns] = low


def started(pairs, sems):
    copies = [pltpu.make_async_copy(source, target, sems.at[n]) for n, (source, target) in enumerate(pairs)]
    for copy in copies:
        copy.start()
    return copies


def inner_kernel(layers, *refs):
    arrays, (below_hbm, above_hbm, store, lo_out, hi_out, below, above, part, lam, along, sems) = refs[:6], refs[6:]
    count = len(layers)
    waits = started([(below_hbm, below), (above_hbm, above)], sems)

    def give_faces():
        lo_out[...] = part[0, pl.ds(0, 576, stride=8), :]
        hi_out[...] = part[count - 1, pl.ds(4, 576, stride=8), :]

    belows = [below] + [None] * (count - 1)
    aboves = [None] * (count - 1) + [above]
    layer_pieces(layers, arrays, waits, belows, aboves, part, lam, along, store, give_faces)


def outer_kernel(last, devices, capacity, *refs):
    arrays, (above_first, below_last, inner), hbm, send_hbm = refs[:6], refs[6:9], refs[9:15], refs[15]
    local, (part, lam, along, store, send, sems) = refs[16:22], refs[22:]
    waits = started(list(zip(hbm, local)), sems)
    below_first, above_last = local[:2]
    layer_pieces(
        (0, last), arrays, waits, [below_first, below_last], [above_first, above_last], part, lam, along, store, lambda: None
    )
    slots, ids = routes(devices, capacity, *local[2:])
    numbers = jnp.concatenate(halves_of(ids), axis=1)
    total = send.shape[0]
    parts = 4 if total % 32 == 0 else 1
    size = total // parts
    outs = []
    for n in range(parts):
        rows = iota((size, CROSS), 0) + n * size

        def chosen(which):
            return jnp.concatenate(
                [onehot(rows == slots[o][:, l * CROSS : (l + 1) * CROSS]) for l in which for o in range(2)], axis=1
            )

        homes = iota((size, devices), 1) * (capacity + 1) + capacity
        numbered = onehot(iota((size, devices), 0) + n * size == homes)
        both = dot_nt(chosen(range(1, last)), inner[...]) + dot_nt(chosen((0, last)), store[...]) + dot(numbered, numbers)
        at = pl.ds(n * size, size)
        send[at, :] = both[:, :128] + both[:, 128:]
        copy = pltpu.make_async_copy(send.at[at], send_hbm.at[at], sems.at[6 + n])
        copy.start()
        outs.append(copy)
    for copy in outs:
        copy.wait()


def gather_kernel(devices, capacity, rows_ref, out_hbm, halves, ids, image, sems):
    total = devices * (capacity + 1)
    wide = halves.shape[0]
    high, low = halves_of(rows_ref[...])
    halves[:total, :128] = high
    halves[:total, 128:] = low
    if wide > total:
        halves[total:, :] = jnp.zeros((wide - total, 256), BF16)
    numbers = rows_ref[pl.ds(capacity, devices, stride=capacity + 1), :]
    column = iota((128, wide), 1)
    spread = onehot(iota((128, wide), 0) == column % (capacity + 1))
    high, low = halves_of(numbers)
    tiled = dot(high, spread) + dot(low, spread)
    at = iota((devices, wide), 1)
    mine = (at // (capacity + 1) == iota((devices, wide), 0)) & (at % (capacity + 1) < capacity)
    found = jnp.sum(jnp.where(mine, tiled + 1.0, 0.0), axis=0, keepdims=True) - 1.0
    ids[...] = found.astype(jnp.int32)
    step = 256
    outs = []
    for n in range(BLOCKS // step):
        named = onehot(iota((step, wide), 0) + n * step == ids[...])
        both = dot(named, halves[...])
        at = pl.ds(n * step, step)
        image[at, :] = both[:, :128] + both[:, 128:]
        copy = pltpu.make_async_copy(image.at[at], out_hbm.at[at], sems.at[n])
        copy.start()
        outs.append(copy)
    for copy in outs:
        copy.wait()


def params():
    return pltpu.CompilerParams(vmem_limit_bytes=24 * 1024 * 1024)


FAR = pl.BlockSpec(memory_space=pltpu.HBM)
NEAR = pl.BlockSpec(memory_space=pltpu.VMEM)


def shards(
    velocity,
    inverse_sizes,
    resample_x,
    resample_y,
    resample_z,
    piece_target,
    target_brick,
    target_block,
    brick_home,
):
    elements = velocity.shape[2]
    last = elements // CROSS - 1
    devices = lax.axis_size("dom")
    capacity = max(2, 4 * elements // devices)
    whole, faces = (jnp.asarray(o) for o in operators())
    face = (576, CROSS)
    face_shape = jax.ShapeDtypeStruct(face, F32)

    lo_first, hi_first, lo_last, hi_last = pl.pallas_call(
        functools.partial(rim_kernel, last),
        in_specs=[FAR] * 3,
        out_specs=[FAR] * 4,
        out_shape=[face_shape] * 4,
        scratch_shapes=[
            pltpu.VMEM(faces.shape, BF16),
            pltpu.VMEM((2, 3, 512, CROSS), BF16),
            pltpu.VMEM((2, 3, CROSS), F32),
            pltpu.VMEM((2, 2) + face, F32),
            pltpu.SemaphoreType.DMA((9,)),
        ],
        compiler_params=params(),
        name="rim_faces",
    )(faces, velocity, inverse_sizes)
    from_prev = lax.ppermute(hi_last, "dom", [(i, (i + 1) % devices) for i in range(devices)])
    from_next = lax.ppermute(lo_first, "dom", [((i + 1) % devices, i) for i in range(devices)])

    arrays = (whole, velocity, inverse_sizes, resample_x, resample_y, resample_z)

    def scratch(count):
        return [
            pltpu.VMEM((count, 4608, CROSS), F32),
            pltpu.VMEM((512, CROSS), F32),
            pltpu.VMEM((2, 256, CROSS), F32),
        ]

    inside = tuple(range(1, last))
    inner, lo_inner, hi_inner = pl.pallas_call(
        functools.partial(inner_kernel, inside),
        in_specs=[NEAR] * 6 + [FAR] * 2,
        out_specs=[NEAR] * 3,
        out_shape=[jax.ShapeDtypeStruct((256, len(inside) * 256), BF16), face_shape, face_shape],
        scratch_shapes=[pltpu.VMEM(face, F32)] * 2 + scratch(len(inside)) + [pltpu.SemaphoreType.DMA((2,))],
        compiler_params=params(),
        name="inner_layers",
    )(*arrays, hi_first, lo_last)

    rows = devices * (capacity + 1)
    routing = (
        piece_target,
        target_brick.reshape(1, elements),
        target_block.reshape(1, elements),
        brick_home.reshape(1, -1),
    )
    sendbuf = pl.pallas_call(
        functools.partial(outer_kernel, last, devices, capacity),
        in_specs=[NEAR] * 9 + [FAR] * 6,
        out_specs=FAR,
        out_shape=jax.ShapeDtypeStruct((rows, 128), F32),
        scratch_shapes=[pltpu.VMEM(face, F32)] * 2
        + [pltpu.VMEM(array.shape, array.dtype) for array in routing]
        + scratch(2)
        + [pltpu.VMEM((256, 512), BF16), pltpu.VMEM((rows, 128), F32), pltpu.SemaphoreType.DMA((10,))],
        compiler_params=params(),
        name="outer_layers",
    )(*arrays, lo_inner, hi_inner, inner, from_prev, from_next, *routing)

    received = lax.all_to_all(
        sendbuf.reshape(devices, 1, (capacity + 1) * 128), "dom", split_axis=0, concat_axis=0, tiled=True
    )
    wide = -(-rows // 128) * 128
    image = pl.pallas_call(
        functools.partial(gather_kernel, devices, capacity),
        in_specs=[NEAR],
        out_specs=FAR,
        out_shape=jax.ShapeDtypeStruct((BLOCKS, 128), F32),
        scratch_shapes=[
            pltpu.VMEM((wide, 256), BF16),
            pltpu.VMEM((1, wide), jnp.int32),
            pltpu.VMEM((BLOCKS, 128), F32),
            pltpu.SemaphoreType.DMA((8,)),
        ],
        compiler_params=params(),
        name="block_sums",
    )(received.reshape(rows, 128))
    return image[None]


def solution(mesh):
    return jax.shard_map(
        shards,
        mesh=mesh,
        in_specs=(
            P(None, None, "dom"),
            P(None, "dom"),
            P(None, None, None, "dom"),
            P(None, None, None, "dom"),
            P(None, None, None, "dom"),
            P(None, "dom"),
            P("dom", None),
            P("dom"),
            P(),
        ),
        out_specs=P("dom", None, None),
        check_vma=False,
    )
```

```python
import functools
import math

import jax
import jax.numpy as jnp
import ml_dtypes
import numpy as np
from jax import lax
from jax.experimental import pallas as pl
from jax.experimental.pallas import tpu as pltpu
from jax.sharding import PartitionSpec as P

EYN = 8
EZN = 16
CROSS = EYN * EZN
BLOCKS = 2048
F32 = jnp.float32
BF16 = jnp.bfloat16

GLL_NODES = [
    -1.0,
    -0.8717401485096066,
    -0.5917001814331423,
    -0.2092992179024789,
    0.2092992179024789,
    0.5917001814331423,
    0.8717401485096066,
    1.0,
]

ORDER = [0, 1, 2, 3, 7, 4, 5, 6]


def derivative_operator():
    barycentric = []
    for first in range(8):
        product_term = 1.0
        for other in range(8):
            if other != first:
                product_term = product_term * (GLL_NODES[first] - GLL_NODES[other])
        barycentric.append(1.0 / product_term)
    matrix_rows = []
    for first in range(8):
        row_values = []
        for second in range(8):
            if second == first:
                row_values.append(0.0)
            else:
                row_values.append(
                    barycentric[second]
                    / barycentric[first]
                    / (GLL_NODES[first] - GLL_NODES[second])
                )
        row_values[first] = -sum(row_values)
        matrix_rows.append(row_values)
    diff_matrix = np.array(matrix_rows)
    identity = np.eye(8)
    return np.concatenate(
        [
            np.kron(np.kron(diff_matrix, identity), identity),
            np.kron(np.kron(identity, diff_matrix), identity),
            np.kron(np.kron(identity, identity), diff_matrix),
        ],
        axis=0,
    )


def operators():
    rounded = derivative_operator().astype(np.float32).astype(ml_dtypes.bfloat16).astype(np.float32)
    ends = np.ones(8, np.float32)
    ends[0] = ends[7] = 0.5
    halves = ends[:, None, None] * ends[None, :, None] * ends[None, None, :]
    rows = rounded.reshape(3, 8, 8, 8, 512) * halves[None, :, :, :, None]
    rows = rows.transpose(0, 2, 3, 1, 4)[:, :, ORDER]
    whole = rows[:, :, :, ORDER].reshape(3, 512, 512)
    faces = np.stack([rows[:, :, :, 0], rows[:, :, :, 7]]).reshape(384, 512)
    return whole.astype(ml_dtypes.bfloat16), faces.astype(ml_dtypes.bfloat16)


def third_angle():
    spots = (1.0 - np.cos(np.pi * (np.arange(4000) + 0.5) / 4000)) / 2
    values = np.sin(np.arcsin(1.0 - spots * spots) / 3.0)
    fitted = np.polynomial.chebyshev.Chebyshev.fit(spots, values, 9, domain=[0, 1])
    return [float(c) for c in fitted.convert(kind=np.polynomial.Polynomial).coef]


THIRD = third_angle()


def dot(left, right):
    return lax.dot_general(left, right, (((1,), (0,)), ((), ())), preferred_element_type=F32)


def dot_nt(left, right):
    return lax.dot_general(left, right, (((1,), (1,)), ((), ())), preferred_element_type=F32)


def iota(shape, axis):
    return lax.broadcasted_iota(jnp.int32, shape, axis)


def onehot(mask):
    return jnp.where(mask, 1.0, 0.0).astype(BF16)


def halves_of(values):
    high = values.astype(BF16)
    return high, (values - high.astype(F32)).astype(BF16)


def normal_sums(low, high):
    normal = iota(low.shape, 1) // EZN
    below = pltpu.roll(high, EZN, 1)
    above = pltpu.roll(low, CROSS - EZN, 1)
    return (
        low + jnp.where(normal == 0, low, below),
        high + jnp.where(normal == EYN - 1, high, above),
    )


def span_lanes(step):
    lane = iota((8, CROSS), 1)
    return lane // EZN * EZN + (lane + step) % EZN


def moved(values, lanes):
    index = jnp.broadcast_to(lanes[None], (values.shape[0] // 8, 8, CROSS)).reshape(values.shape)
    return jnp.take_along_axis(values, index, axis=1, mode="promise_in_bounds")


def rim_kernel(last, faces, vel, sizes, lo_first, hi_last):
    sub = iota((64, CROSS), 0) % 8
    before, after = span_lanes(EZN - 1), span_lanes(1)
    for face, l, out in ((1, last, hi_last), (0, 0, lo_first)):
        lanes = slice(l * CROSS, (l + 1) * CROSS)
        for c in range(3):
            products = dot(faces[face * 192 : face * 192 + 192, :], vel[c, :, lanes])
            for a in range(3):
                part = products[a * 64 : a * 64 + 64] * sizes[a : a + 1, lanes]
                low, high = normal_sums(part[:8], part[56:])
                part = jnp.concatenate([low, part[8:56], high], axis=0)
                swapped = jnp.where(sub == 0, moved(part, after), moved(part, before))
                swapped = pltpu.roll(swapped.reshape(8, 8, CROSS), 4, 1).reshape(64, CROSS)
                part = part + jnp.where((sub == 0) | (sub == 4), swapped, 0.0)
                out[pl.ds((c * 3 + a) * 64, 64), :] = part


def routes(devices, capacity, pt_ref, brick_ref, block_ref, home_ref):
    targets = brick_ref.shape[1]
    bricks = home_ref.shape[1]
    named = jnp.where(iota((bricks, targets), 0) == brick_ref[...], 1.0, 0.0)
    earlier = onehot(iota((targets, targets), 0) < iota((targets, targets), 1))
    ranks = dot(named.astype(BF16), earlier)
    homes = jnp.broadcast_to(home_ref[...].astype(F32), (8, bricks)).astype(BF16)
    owner = dot(homes, named.astype(BF16))[0:1]
    rank = jnp.sum(named * ranks, axis=0, keepdims=True)
    row = iota((8, targets), 0)
    both = jnp.where(row == 0, owner, jnp.where(row == 1, rank, 0.0)).astype(BF16)
    slots = []
    for o in range(2):
        picked = onehot(iota((targets, targets), 0) == pt_ref[o : o + 1, :])
        found = dot(both, picked)
        slots.append((found[0:1] * (capacity + 1) + found[1:2]).astype(jnp.int32))
    owned = jnp.where(iota((devices, targets), 0) == owner.astype(jnp.int32), 1.0, 0.0)
    placed = onehot(iota((128, targets), 0) == rank.astype(jnp.int32))
    block = block_ref[...]
    upper = (block // 64).astype(F32)
    lower = (block % 64).astype(F32)
    ids = (
        dot_nt((owned * upper).astype(BF16), placed) * 64.0
        + dot_nt((owned * lower).astype(BF16), placed)
        + dot_nt(owned.astype(BF16), placed)
        - 1.0
    )
    return slots, ids


def middle_eigen(g):
    s01, s02, s12 = g[0][1] + g[1][0], g[0][2] + g[2][0], g[1][2] + g[2][1]
    p01, p02, p12 = g[0][1] * g[1][0], g[0][2] * g[2][0], g[1][2] * g[2][1]
    m00 = g[0][0] * g[0][0] + (p01 + p02)
    m11 = g[1][1] * g[1][1] + (p01 + p12)
    m22 = g[2][2] * g[2][2] + (p02 + p12)
    m01 = 0.5 * ((g[0][0] + g[1][1]) * s01 + (g[0][2] * g[2][1] + g[1][2] * g[2][0]))
    m02 = 0.5 * ((g[0][0] + g[2][2]) * s02 + (g[0][1] * g[1][2] + g[2][1] * g[1][0]))
    m12 = 0.5 * ((g[1][1] + g[2][2]) * s12 + (g[1][0] * g[0][2] + g[2][0] * g[0][1]))
    q = (m00 + m11 + m22) * (1.0 / 3.0)
    x, y, z = m00 - q, m11 - q, m22 - q
    n01, n02, n12 = m01 * m01, m02 * m02, m12 * m12
    spread = (x * x + y * y + z * z + 2.0 * (n01 + n02 + n12)) * (1.0 / 6.0)
    halfdet = 0.5 * (x * (y * z - n12) - z * n01 - y * n02) + m01 * m02 * m12
    inverse = lax.rsqrt(jnp.maximum(spread, 1e-37))
    ratio = ((jnp.abs(halfdet) * inverse) * inverse) * inverse
    gap = jnp.maximum(1.0 - ratio, 1e-30)
    root = gap * lax.rsqrt(gap)
    pairs = [THIRD[n] + THIRD[n + 1] * root for n in range(0, 10, 2)]
    square = root * root
    fourth = square * square
    third = (pairs[0] + pairs[1] * square) + fourth * (
        (pairs[2] + pairs[3] * square) + fourth * pairs[4]
    )
    turn = 2.0 * (spread * inverse) * third
    return jnp.where(halfdet < 0.0, q + turn, q - turn)


def resample_layer(lam, l, lanes, rx, ry, rz, along, store, at):
    for o in range(2):
        for j in range(8):
            rows = [lam[l, pl.ds((j * 8 + k) * 8, 8), :] for k in range(8)]
            for w in range(4):
                total = rows[0] * rz[o, w, ORDER[0] : ORDER[0] + 1, lanes]
                for k in range(1, 8):
                    total = total + rows[k] * rz[o, w, ORDER[k] : ORDER[k] + 1, lanes]
                along[0, pl.ds((w * 8 + j) * 8, 8), :] = total
        for w in range(4):
            rows = [along[0, pl.ds((w * 8 + j) * 8, 8), :] for j in range(8)]
            for v in range(4):
                total = rows[0] * ry[o, v, 0:1, lanes]
                for j in range(1, 8):
                    total = total + rows[j] * ry[o, v, j : j + 1, lanes]
                along[1, pl.ds((v * 4 + w) * 8, 8), :] = total
        rows = [along[1, pl.ds(i, 16, stride=8), :] for i in range(8)]
        for u in range(8):
            total = rows[0] * rx[o, u, ORDER[0] : ORDER[0] + 1, lanes]
            for i in range(1, 8):
                total = total + rows[i] * rx[o, u, ORDER[i] : ORDER[i] + 1, lanes]
            high, low = halves_of(total)
            columns = pl.ds((at * 2 + o) * CROSS, CROSS)
            store[pl.ds(u * 16, 16), columns] = high
            store[pl.ds(128 + u * 16, 16), columns] = low


def started(pairs, sems):
    copies = [pltpu.make_async_copy(source, target, sems.at[n]) for n, (source, target) in enumerate(pairs)]
    for copy in copies:
        copy.start()
    return copies


def layer_lanes(l):
    return slice(l * CROSS, (l + 1) * CROSS)


def inner_kernel(layers, op, vel, sizes, rx, ry, rz, store, lam_ends, lo_first, hi_last, part, lam, along):
    last = layers - 1
    before, after = span_lanes(EZN - 1), span_lanes(1)
    for c in range(3):
        for a in range(3):
            products = dot(op[a], vel[c]) * sizes[a : a + 1, :]
            for l in range(layers):
                values = products[:, layer_lanes(l)]
                first, final = normal_sums(values[:64], values[448:])
                for j in range(8):
                    rows = {0: first, 7: final}.get(j, values[j * 64 : (j + 1) * 64])
                    near, far = rows[:8], rows[32:40]
                    at = (c * 3 + a) * 512 + j * 64
                    part[l, pl.ds(at, 8), :] = near + moved(far, before)
                    part[l, pl.ds(at + 8, 24), :] = rows[8:32]
                    part[l, pl.ds(at + 32, 8), :] = far + moved(near, after)
                    part[l, pl.ds(at + 40, 24), :] = rows[40:]

    def face_sums(ca, carry):
        near, far = pl.ds(ca * 512, 64, stride=8), pl.ds(ca * 512 + 4, 64, stride=8)
        for l in range(last):
            shared = part[l, far, :] + part[l + 1, near, :]
            part[l, far, :] = shared
            part[l + 1, near, :] = shared
        rows = pl.ds(ca * 64, 64)
        lo_first[rows, :] = part[0, near, :]
        hi_last[rows, :] = part[last, far, :]
        return carry

    lax.fori_loop(0, 9, face_sums, 0, unroll=3)

    def eigen(l, target, n):
        def point_row(jk, carry):
            g = [part[l, pl.ds(ca * 512 + jk * 8, 8), :] for ca in range(9)]
            target[n, pl.ds(jk * 8, 8), :] = middle_eigen([g[0:3], g[3:6], g[6:9]])
            return carry

        lax.fori_loop(0, 64, point_row, 0, unroll=16)

    for l in range(layers):
        if l in (0, last):
            eigen(l, lam_ends, min(l, 1))
        else:
            eigen(l, lam, 0)
            resample_layer(lam, 0, layer_lanes(l), rx, ry, rz, along, store, l - 1)


def outer_kernel(last, devices, capacity, *refs):
    (rx, ry, rz, lam_ends, lo_first, hi_last, inner), hbm, send_hbm = refs[:7], refs[7:13], refs[13]
    local, (lam, along, store, send, sems) = refs[14:20], refs[20:]
    waits = started(list(zip(hbm, local)), sems)
    lam[...] = lam_ends[...]
    for copy in waits:
        copy.wait()
    for n, own, other, at in ((0, lo_first, local[0], 0), (1, hi_last, local[1], 4)):
        g = [own[ca * 64 : ca * 64 + 64, :] + other[ca * 64 : ca * 64 + 64, :] for ca in range(9)]
        lam[n, pl.ds(at, 64, stride=8), :] = middle_eigen([g[0:3], g[3:6], g[6:9]])
    for n, l in ((0, 0), (1, last)):
        resample_layer(lam, n, layer_lanes(l), rx, ry, rz, along, store, n)
    slots, ids = routes(devices, capacity, *local[2:])
    numbers = jnp.concatenate(halves_of(ids), axis=1)
    total = send.shape[0]
    parts = 4 if total % 32 == 0 else 1
    size = total // parts
    outs = []
    for n in range(parts):
        rows = iota((size, CROSS), 0) + n * size

        def chosen(which):
            return jnp.concatenate([onehot(rows == slots[o][:, layer_lanes(l)]) for l in which for o in range(2)], axis=1)

        homes = iota((size, devices), 1) * (capacity + 1) + capacity
        numbered = onehot(iota((size, devices), 0) + n * size == homes)
        both = dot_nt(chosen(range(1, last)), inner[...]) + dot_nt(chosen((0, last)), store[...]) + dot(numbered, numbers)
        at = pl.ds(n * size, size)
        send[at, :] = both[:, :128] + both[:, 128:]
        copy = pltpu.make_async_copy(send.at[at], send_hbm.at[at], sems.at[6 + n])
        copy.start()
        outs.append(copy)
    for copy in outs:
        copy.wait()


def gather_kernel(devices, capacity, rows_ref, out_hbm, halves, ids, image, sems):
    total = devices * (capacity + 1)
    wide = halves.shape[0]
    high, low = halves_of(rows_ref[...])
    halves[:total, :128] = high
    halves[:total, 128:] = low
    if wide > total:
        halves[total:, :] = jnp.zeros((wide - total, 256), BF16)
    numbers = rows_ref[pl.ds(capacity, devices, stride=capacity + 1), :]
    column = iota((128, wide), 1)
    spread = onehot(iota((128, wide), 0) == column % (capacity + 1))
    high, low = halves_of(numbers)
    tiled = dot(high, spread) + dot(low, spread)
    at = iota((devices, wide), 1)
    mine = (at // (capacity + 1) == iota((devices, wide), 0)) & (at % (capacity + 1) < capacity)
    found = jnp.sum(jnp.where(mine, tiled + 1.0, 0.0), axis=0, keepdims=True) - 1.0
    ids[...] = found.astype(jnp.int32)
    step = 256
    outs = []
    for n in range(BLOCKS // step):
        named = onehot(iota((step, wide), 0) + n * step == ids[...])
        both = dot(named, halves[...])
        at = pl.ds(n * step, step)
        image[at, :] = both[:, :128] + both[:, 128:]
        copy = pltpu.make_async_copy(image.at[at], out_hbm.at[at], sems.at[n])
        copy.start()
        outs.append(copy)
    for copy in outs:
        copy.wait()


def kernel_call(kernel, name, micros, megabytes=24, **rest):
    return pl.pallas_call(
        kernel,
        name=name,
        cost_estimate=pl.CostEstimate(flops=int(micros * 1e9), bytes_accessed=0, transcendentals=0),
        compiler_params=pltpu.CompilerParams(vmem_limit_bytes=megabytes * 1024 * 1024),
        **rest,
    )


FAR = pl.BlockSpec(memory_space=pltpu.HBM)
NEAR = pl.BlockSpec(memory_space=pltpu.VMEM)


def shards(
    velocity,
    inverse_sizes,
    resample_x,
    resample_y,
    resample_z,
    piece_target,
    target_brick,
    target_block,
    brick_home,
):
    elements = velocity.shape[2]
    last = elements // CROSS - 1
    devices = lax.axis_size("dom")
    capacity = max(2, 4 * elements // devices)
    whole, faces = (jnp.asarray(o) for o in operators())
    layers = last + 1
    face = (576, CROSS)
    face_shape = jax.ShapeDtypeStruct(face, F32)
    ends_shape = jax.ShapeDtypeStruct((2, 512, CROSS), F32)

    rim_lo, rim_hi = kernel_call(
        functools.partial(rim_kernel, last),
        "rim_faces",
        3,
        in_specs=[NEAR] * 3,
        out_specs=[NEAR] * 2,
        out_shape=[face_shape] * 2,
    )(faces, velocity, inverse_sizes)
    from_prev = lax.ppermute(rim_hi, "dom", [(i, (i + 1) % devices) for i in range(devices)])
    from_next = lax.ppermute(rim_lo, "dom", [((i + 1) % devices, i) for i in range(devices)])

    weights = (resample_x, resample_y, resample_z)
    along = pltpu.VMEM((2, 256, CROSS), F32)
    inner, lam_ends, lo_first, hi_last = kernel_call(
        functools.partial(inner_kernel, layers),
        "inner_layers",
        9,
        in_specs=[NEAR] * 6,
        out_specs=[NEAR] * 4,
        out_shape=[jax.ShapeDtypeStruct((256, (layers - 2) * 256), BF16), ends_shape, face_shape, face_shape],
        scratch_shapes=[
            pltpu.VMEM((layers, 4608, CROSS), F32),
            pltpu.VMEM((1, 512, CROSS), F32),
            along,
        ],
    )(whole, velocity, inverse_sizes, *weights)

    rows = devices * (capacity + 1)
    routing = (
        piece_target,
        target_brick.reshape(1, elements),
        target_block.reshape(1, elements),
        brick_home.reshape(1, -1),
    )
    sendbuf = kernel_call(
        functools.partial(outer_kernel, last, devices, capacity),
        "outer_layers",
        5,
        in_specs=[NEAR] * 7 + [FAR] * 6,
        out_specs=FAR,
        out_shape=jax.ShapeDtypeStruct((rows, 128), F32),
        scratch_shapes=[pltpu.VMEM(face, F32)] * 2
        + [pltpu.VMEM(array.shape, array.dtype) for array in routing]
        + [
            pltpu.VMEM(ends_shape.shape, F32),
            along,
            pltpu.VMEM((256, 512), BF16),
            pltpu.VMEM((rows, 128), F32),
            pltpu.SemaphoreType.DMA((10,)),
        ],
    )(*weights, lam_ends, lo_first, hi_last, inner, from_prev, from_next, *routing)

    received = lax.all_to_all(
        sendbuf.reshape(devices, 1, (capacity + 1) * 128), "dom", split_axis=0, concat_axis=0, tiled=True
    )
    wide = -(-rows // 128) * 128
    image = kernel_call(
        functools.partial(gather_kernel, devices, capacity),
        "block_sums",
        4,
        in_specs=[NEAR],
        out_specs=FAR,
        out_shape=jax.ShapeDtypeStruct((BLOCKS, 128), F32),
        scratch_shapes=[
            pltpu.VMEM((wide, 256), BF16),
            pltpu.VMEM((1, wide), jnp.int32),
            pltpu.VMEM((BLOCKS, 128), F32),
            pltpu.SemaphoreType.DMA((8,)),
        ],
    )(received.reshape(rows, 128))
    return image[None]


def solution(mesh):
    return jax.shard_map(
        shards,
        mesh=mesh,
        in_specs=(
            P(None, None, "dom"),
            P(None, "dom"),
            P(None, None, None, "dom"),
            P(None, None, None, "dom"),
            P(None, None, None, "dom"),
            P(None, "dom"),
            P("dom", None),
            P("dom"),
            P(),
        ),
        out_specs=P("dom", None, None),
        check_vma=False,
    )
```

```python
import functools
import math

import jax
import jax.numpy as jnp
import ml_dtypes
import numpy as np
from jax import lax
from jax.experimental import pallas as pl
from jax.experimental.pallas import tpu as pltpu
from jax.sharding import PartitionSpec as P

EYN = 8
EZN = 16
CROSS = EYN * EZN
BLOCKS = 2048
F32 = jnp.float32
BF16 = jnp.bfloat16

GLL_NODES = [
    -1.0,
    -0.8717401485096066,
    -0.5917001814331423,
    -0.2092992179024789,
    0.2092992179024789,
    0.5917001814331423,
    0.8717401485096066,
    1.0,
]

ORDER = [0, 1, 2, 3, 7, 4, 5, 6]


def derivative_matrix():
    barycentric = []
    for first in range(8):
        product_term = 1.0
        for other in range(8):
            if other != first:
                product_term = product_term * (GLL_NODES[first] - GLL_NODES[other])
        barycentric.append(1.0 / product_term)
    matrix_rows = []
    for first in range(8):
        row_values = []
        for second in range(8):
            if second == first:
                row_values.append(0.0)
            else:
                row_values.append(
                    barycentric[second]
                    / barycentric[first]
                    / (GLL_NODES[first] - GLL_NODES[second])
                )
        row_values[first] = -sum(row_values)
        matrix_rows.append(row_values)
    diff_matrix = np.array(matrix_rows)
    return diff_matrix


def rounded_matrix():
    return derivative_matrix().astype(np.float32).astype(ml_dtypes.bfloat16).astype(np.float32)


def operator_rows():
    matrix, identity = rounded_matrix(), np.eye(8, dtype=np.float32)
    whole = np.stack(
        [
            np.kron(np.kron(matrix, identity), identity),
            np.kron(np.kron(identity, matrix), identity),
            np.kron(np.kron(identity, identity), matrix),
        ]
    )
    ends = np.ones(8, np.float32)
    ends[0] = ends[7] = 0.5
    halves = ends[:, None, None] * ends[None, :, None] * ends[None, None, :]
    rows = whole.reshape(3, 8, 8, 8, 512) * halves[None, :, :, :, None]
    rows = rows.transpose(0, 2, 3, 1, 4)[:, :, :, ORDER].reshape(3, 512, 512)
    split = rows[::2].reshape(2, 2, 256, 8, 2, 32)
    blocks = np.stack([split[:, half, :, :, half, :].reshape(2, 256, 256) for half in range(2)], axis=1)
    return rows[1].astype(ml_dtypes.bfloat16), blocks.astype(ml_dtypes.bfloat16)


MATRIX = rounded_matrix()


def third_angle():
    spots = (1.0 - np.cos(np.pi * (np.arange(4000) + 0.5) / 4000)) / 2
    values = np.sin(np.arcsin(1.0 - spots * spots) / 3.0)
    fitted = np.polynomial.chebyshev.Chebyshev.fit(spots, values, 8, domain=[0, 1])
    return [2.0 / math.sqrt(3.0) * float(c) for c in fitted.convert(kind=np.polynomial.Polynomial).coef]


THIRD = third_angle()


def dot(left, right):
    return lax.dot_general(left, right, (((1,), (0,)), ((), ())), preferred_element_type=F32)


def dot_nt(left, right):
    return lax.dot_general(left, right, (((1,), (1,)), ((), ())), preferred_element_type=F32)


def iota(shape, axis):
    return lax.broadcasted_iota(jnp.int32, shape, axis)


def onehot(mask):
    return jnp.where(mask, 1.0, 0.0).astype(BF16)


def halves_of(values):
    high = values.astype(BF16)
    return high, (values - high.astype(F32)).astype(BF16)


def normal_sums(low, high):
    normal = iota(low.shape, 1) // EZN
    below = pltpu.roll(high, EZN, 1)
    above = pltpu.roll(low, CROSS - EZN, 1)
    return (
        low + jnp.where(normal == 0, low, below),
        high + jnp.where(normal == EYN - 1, high, above),
    )


def span_lanes(step):
    lane = iota((8, CROSS), 1)
    return lane // EZN * EZN + (lane + step) % EZN


def moved(values, lanes):
    index = jnp.broadcast_to(lanes[None], (values.shape[0] // 8, 8, CROSS)).reshape(values.shape)
    return jnp.take_along_axis(values, index, axis=1, mode="promise_in_bounds")


def rim_kernel(last, vel, sizes, lo_first, hi_last):
    sub = iota((8, CROSS), 0)
    before, after = span_lanes(EZN - 1), span_lanes(1)
    ends = jnp.where((sub == 0) | (sub == 7), 0.5, 1.0)
    turned = []
    for shift in range(8):
        column = jnp.zeros((8, CROSS), F32)
        for k in range(8):
            column = jnp.where(sub == k, float(MATRIX[k, (k - shift) % 8]), column)
        turned.append(column)
    for end, l, out in ((7, last, hi_last), (0, 0, lo_first)):
        lanes = layer_lanes(l)
        for c in range(3):
            line = [vel[c, i * 64 : i * 64 + 64, lanes].astype(F32) for i in range(8)]
            along_x = line[0] * float(MATRIX[end, 0])
            for i in range(1, 8):
                along_x = along_x + line[i] * float(MATRIX[end, i])
            face = [line[end][j * 8 : j * 8 + 8] for j in range(8)]
            along_y, along_z = [], []
            for j in range(8):
                total = face[0] * float(MATRIX[j, 0])
                for other in range(1, 8):
                    total = total + face[other] * float(MATRIX[j, other])
                along_y.append(total)
                total = face[j] * turned[0]
                for shift in range(1, 8):
                    total = total + pltpu.roll(face[j], shift, 0) * turned[shift]
                along_z.append(total)
            for a, rows in enumerate(([along_x[j * 8 : j * 8 + 8] for j in range(8)], along_y, along_z)):
                scale = sizes[a : a + 1, lanes] * (0.5 * ends)
                rows = [row * scale for row in rows]
                rows[0], rows[7] = normal_sums(rows[0] * 0.5, rows[7] * 0.5)
                for j in range(8):
                    low = pltpu.roll(moved(rows[j], before), 1, 0)
                    high = pltpu.roll(moved(rows[j], after), 7, 0)
                    shared = rows[j] + jnp.where(sub == 0, low, jnp.where(sub == 7, high, 0.0))
                    out[pl.ds(((c * 3 + a) * 8 + j) * 8, 8), :] = shared


def routes(devices, capacity, pt_ref, brick_ref, block_ref, home_ref):
    targets = brick_ref.shape[1]
    bricks = home_ref.shape[1]
    named = jnp.where(iota((bricks, targets), 0) == brick_ref[...], 1.0, 0.0)
    earlier = onehot(iota((targets, targets), 0) < iota((targets, targets), 1))
    ranks = dot(named.astype(BF16), earlier)
    homes = jnp.broadcast_to(home_ref[...].astype(F32), (8, bricks)).astype(BF16)
    owner = dot(homes, named.astype(BF16))[0:1]
    rank = jnp.sum(named * ranks, axis=0, keepdims=True)
    row = iota((8, targets), 0)
    both = jnp.where(row == 0, owner, jnp.where(row == 1, rank, 0.0)).astype(BF16)
    slots = []
    for o in range(2):
        picked = onehot(iota((targets, targets), 0) == pt_ref[o : o + 1, :])
        found = dot(both, picked)
        slots.append((found[0:1] * (capacity + 1) + found[1:2]).astype(jnp.int32))
    owned = jnp.where(iota((devices, targets), 0) == owner.astype(jnp.int32), 1.0, 0.0)
    placed = onehot(iota((128, targets), 0) == rank.astype(jnp.int32))
    block = block_ref[...]
    upper = (block // 64).astype(F32)
    lower = (block % 64).astype(F32)
    ids = (
        dot_nt((owned * upper).astype(BF16), placed) * 64.0
        + dot_nt((owned * lower).astype(BF16), placed)
        + dot_nt(owned.astype(BF16), placed)
        - 1.0
    )
    return slots, ids


def middle_eigen(g):
    s01, s02, s12 = g[0][1] + g[1][0], g[0][2] + g[2][0], g[1][2] + g[2][1]
    p01, p02, p12 = g[0][1] * g[1][0], g[0][2] * g[2][0], g[1][2] * g[2][1]
    d0, d1, d2 = g[0][0] * g[0][0] - p12, g[1][1] * g[1][1] - p02, g[2][2] * g[2][2] - p01
    mean = (d0 + d1 + d2) * (1.0 / 3.0)
    x, y, z = d0 - mean, d1 - mean, d2 - mean
    q = mean + (p01 + p02 + p12)
    o01 = (g[0][0] + g[1][1]) * s01 + (g[0][2] * g[2][1] + g[1][2] * g[2][0])
    o02 = (g[0][0] + g[2][2]) * s02 + (g[0][1] * g[1][2] + g[2][1] * g[1][0])
    o12 = (g[1][1] + g[2][2]) * s12 + (g[1][0] * g[0][2] + g[2][0] * g[0][1])
    n01, n02, n12 = o01 * o01, o02 * o02, o12 * o12
    spread = (y * y - x * z) + 0.25 * (n01 + n02 + n12)
    det = 4.0 * (x * y * z) + (o01 * o02 * o12 - (x * n12 + z * n01 + y * n02))
    inverse = lax.rsqrt(jnp.maximum(spread, 1e-37))
    ratio = ((jnp.abs(det) * inverse) * inverse) * (inverse * (3.0 * math.sqrt(3.0) / 8.0))
    gap = jnp.maximum(1.0 - ratio, 1e-30)
    root = gap * lax.rsqrt(gap)
    third = THIRD[-1]
    for coefficient in THIRD[-2::-1]:
        third = third * root + coefficient
    turn = (spread * inverse) * third
    return jnp.where(det < 0.0, q + turn, q - turn)


def resample_layer(lam, l, lanes, rx, ry, rz, along, store, at):
    for o in range(2):
        for j in range(8):
            rows = [lam[l, pl.ds((j * 8 + k) * 8, 8), :] for k in range(8)]
            for w in range(4):
                total = rows[0] * rz[o, w, 0:1, lanes]
                for k in range(1, 8):
                    total = total + rows[k] * rz[o, w, k : k + 1, lanes]
                along[0, pl.ds((w * 8 + j) * 8, 8), :] = total
        for w in range(4):
            rows = [along[0, pl.ds((w * 8 + j) * 8, 8), :] for j in range(8)]
            for v in range(4):
                total = rows[0] * ry[o, v, 0:1, lanes]
                for j in range(1, 8):
                    total = total + rows[j] * ry[o, v, j : j + 1, lanes]
                along[1, pl.ds((v * 4 + w) * 8, 8), :] = total
        rows = [along[1, pl.ds(i, 16, stride=8), :] for i in range(8)]
        for u in range(8):
            total = rows[0] * rx[o, u, ORDER[0] : ORDER[0] + 1, lanes]
            for i in range(1, 8):
                total = total + rows[i] * rx[o, u, ORDER[i] : ORDER[i] + 1, lanes]
            high, low = halves_of(total)
            columns = pl.ds((at * 2 + o) * CROSS, CROSS)
            store[pl.ds(u * 16, 16), columns] = high
            store[pl.ds(128 + u * 16, 16), columns] = low


def started(pairs, sems):
    copies = [pltpu.make_async_copy(source, target, sems.at[n]) for n, (source, target) in enumerate(pairs)]
    for copy in copies:
        copy.start()
    return copies


def layer_lanes(l):
    return slice(l * CROSS, (l + 1) * CROSS)


def inner_kernel(layers, across, blocks, vel, sizes, rx, ry, rz, store, lam_ends, lo_first, hi_last, part, lam, along):
    last = layers - 1
    before, after = span_lanes(EZN - 1), span_lanes(1)
    for c in range(3):
        halves = [
            jnp.concatenate([vel[c, i * 64 + half * 32 : i * 64 + half * 32 + 32, :] for i in range(8)], axis=0)
            for half in range(2)
        ]
        for a in range(3):
            if a == 1:
                products = dot(across[...], vel[c])
            else:
                products = jnp.concatenate([dot(blocks[a // 2, half], halves[half]) for half in range(2)], axis=0)
            products = products * sizes[a : a + 1, :]
            for l in range(layers):
                values = products[:, layer_lanes(l)]
                first, final = normal_sums(values[:64], values[448:])
                for j in range(8):
                    rows = {0: first, 7: final}.get(j, values[j * 64 : (j + 1) * 64])
                    near, far = rows[:8], rows[56:]
                    at = (c * 3 + a) * 512 + j * 64
                    part[l, pl.ds(at, 8), :] = near + moved(far, before)
                    part[l, pl.ds(at + 8, 48), :] = rows[8:56]
                    part[l, pl.ds(at + 56, 8), :] = far + moved(near, after)

    def face_sums(ca, carry):
        near, far = pl.ds(ca * 512, 64, stride=8), pl.ds(ca * 512 + 4, 64, stride=8)
        for l in range(last):
            shared = part[l, far, :] + part[l + 1, near, :]
            part[l, far, :] = shared
            part[l + 1, near, :] = shared
        rows = pl.ds(ca * 64, 64)
        lo_first[rows, :] = part[0, near, :]
        hi_last[rows, :] = part[last, far, :]
        return carry

    lax.fori_loop(0, 9, face_sums, 0, unroll=3)

    def eigen(l, target, n):
        for jk in range(64):
            g = [part[l, pl.ds(ca * 512 + jk * 8, 8), :] for ca in range(9)]
            target[n, pl.ds(jk * 8, 8), :] = middle_eigen([g[0:3], g[3:6], g[6:9]])

    for l in range(layers):
        if l in (0, last):
            eigen(l, lam_ends, min(l, 1))
        else:
            eigen(l, lam, 0)
            resample_layer(lam, 0, layer_lanes(l), rx, ry, rz, along, store, l - 1)


def outer_kernel(last, devices, capacity, *refs):
    (rx, ry, rz, lam_ends, lo_first, hi_last, inner), hbm, send = refs[:7], refs[7:13], refs[13]
    local, (lam, along, store, sems) = refs[14:20], refs[20:]
    waits = started(list(zip(hbm, local)), sems)
    lam[...] = lam_ends[...]
    for copy in waits:
        copy.wait()
    for n, own, other, at in ((0, lo_first, local[0], 0), (1, hi_last, local[1], 4)):
        g = [own[ca * 64 : ca * 64 + 64, :] + other[ca * 64 : ca * 64 + 64, :] for ca in range(9)]
        lam[n, pl.ds(at, 64, stride=8), :] = middle_eigen([g[0:3], g[3:6], g[6:9]])
    for n, l in ((0, 0), (1, last)):
        resample_layer(lam, n, layer_lanes(l), rx, ry, rz, along, store, n)
    slots, ids = routes(devices, capacity, *local[2:])
    numbers = jnp.concatenate(halves_of(ids), axis=1)
    total = send.shape[0]
    parts = 4 if total % 32 == 0 else 1
    size = total // parts
    for n in range(parts):
        rows = iota((size, CROSS), 0) + n * size

        def chosen(which):
            return jnp.concatenate([onehot(rows == slots[o][:, layer_lanes(l)]) for l in which for o in range(2)], axis=1)

        homes = iota((size, devices), 1) * (capacity + 1) + capacity
        numbered = onehot(iota((size, devices), 0) + n * size == homes)
        both = dot_nt(chosen(range(1, last)), inner[...]) + dot_nt(chosen((0, last)), store[...]) + dot(numbered, numbers)
        send[pl.ds(n * size, size), :] = both[:, :128] + both[:, 128:]


def gather_kernel(devices, capacity, rows_ref, out_hbm, halves, ids, image, sems):
    total = devices * capacity
    for n in range(devices):
        high, low = halves_of(rows_ref[pl.ds(n * (capacity + 1), capacity), :])
        halves[pl.ds(n * capacity, capacity), :] = jnp.concatenate([high, low], axis=1)
    numbers = rows_ref[pl.ds(capacity, devices, stride=capacity + 1), :]
    spread = onehot(iota((128, total), 0) == iota((128, total), 1) % capacity)
    high, low = halves_of(numbers)
    tiled = dot(high, spread) + dot(low, spread)
    mine = iota((devices, total), 1) // capacity == iota((devices, total), 0)
    found = jnp.sum(jnp.where(mine, tiled + 1.0, 0.0), axis=0, keepdims=True) - 1.0
    ids[...] = found.astype(jnp.int32)
    step = 256
    outs = []
    for n in range(BLOCKS // step):
        named = onehot(iota((step, total), 0) + n * step == ids[...])
        both = dot(named, halves[...])
        at = pl.ds(n * step, step)
        image[at, :] = both[:, :128] + both[:, 128:]
        copy = pltpu.make_async_copy(image.at[at], out_hbm.at[at], sems.at[n])
        copy.start()
        outs.append(copy)
    for copy in outs:
        copy.wait()


def kernel_call(kernel, name, micros, megabytes=24, **rest):
    return pl.pallas_call(
        kernel,
        name=name,
        cost_estimate=pl.CostEstimate(flops=int(micros * 1e9), bytes_accessed=0, transcendentals=0),
        compiler_params=pltpu.CompilerParams(vmem_limit_bytes=megabytes * 1024 * 1024),
        **rest,
    )


FAR = pl.BlockSpec(memory_space=pltpu.HBM)
NEAR = pl.BlockSpec(memory_space=pltpu.VMEM)


def shards(
    velocity,
    inverse_sizes,
    resample_x,
    resample_y,
    resample_z,
    piece_target,
    target_brick,
    target_block,
    brick_home,
):
    elements = velocity.shape[2]
    last = elements // CROSS - 1
    devices = lax.axis_size("dom")
    capacity = max(2, 4 * elements // devices)
    across, blocks = (jnp.asarray(o) for o in operator_rows())
    layers = last + 1
    face = (576, CROSS)
    face_shape = jax.ShapeDtypeStruct(face, F32)
    ends_shape = jax.ShapeDtypeStruct((2, 512, CROSS), F32)

    rim_lo, rim_hi = kernel_call(
        functools.partial(rim_kernel, last),
        "rim_faces",
        3,
        in_specs=[NEAR] * 2,
        out_specs=[NEAR] * 2,
        out_shape=[face_shape] * 2,
    )(velocity, inverse_sizes)
    from_prev = lax.ppermute(rim_hi, "dom", [(i, (i + 1) % devices) for i in range(devices)])
    from_next = lax.ppermute(rim_lo, "dom", [((i + 1) % devices, i) for i in range(devices)])

    weights = (resample_x, resample_y, resample_z)
    along = pltpu.VMEM((2, 256, CROSS), F32)
    inner, lam_ends, lo_first, hi_last = kernel_call(
        functools.partial(inner_kernel, layers),
        "inner_layers",
        8,
        in_specs=[NEAR] * 7,
        out_specs=[NEAR] * 4,
        out_shape=[jax.ShapeDtypeStruct((256, (layers - 2) * 256), BF16), ends_shape, face_shape, face_shape],
        scratch_shapes=[
            pltpu.VMEM((layers, 4608, CROSS), F32),
            pltpu.VMEM((1, 512, CROSS), F32),
            along,
        ],
    )(across, blocks, velocity, inverse_sizes, *weights)

    rows = devices * (capacity + 1)
    routing = (
        piece_target,
        target_brick.reshape(1, elements),
        target_block.reshape(1, elements),
        brick_home.reshape(1, -1),
    )
    sendbuf = kernel_call(
        functools.partial(outer_kernel, last, devices, capacity),
        "outer_layers",
        5,
        in_specs=[NEAR] * 7 + [FAR] * 6,
        out_specs=NEAR,
        out_shape=jax.ShapeDtypeStruct((rows, 128), F32),
        scratch_shapes=[pltpu.VMEM(face, F32)] * 2
        + [pltpu.VMEM(array.shape, array.dtype) for array in routing]
        + [
            pltpu.VMEM(ends_shape.shape, F32),
            along,
            pltpu.VMEM((256, 512), BF16),
            pltpu.SemaphoreType.DMA((6,)),
        ],
    )(*weights, lam_ends, lo_first, hi_last, inner, from_prev, from_next, *routing)

    received = lax.all_to_all(
        sendbuf.reshape(devices, 1, (capacity + 1) * 128), "dom", split_axis=0, concat_axis=0, tiled=True
    )
    image = kernel_call(
        functools.partial(gather_kernel, devices, capacity),
        "block_sums",
        4,
        in_specs=[NEAR],
        out_specs=FAR,
        out_shape=jax.ShapeDtypeStruct((BLOCKS, 128), F32),
        scratch_shapes=[
            pltpu.VMEM((devices * capacity, 256), BF16),
            pltpu.VMEM((1, devices * capacity), jnp.int32),
            pltpu.VMEM((BLOCKS, 128), F32),
            pltpu.SemaphoreType.DMA((8,)),
        ],
    )(received.reshape(rows, 128))
    return image[None]


def solution(mesh):
    return jax.shard_map(
        shards,
        mesh=mesh,
        in_specs=(
            P(None, None, "dom"),
            P(None, "dom"),
            P(None, None, None, "dom"),
            P(None, None, None, "dom"),
            P(None, None, None, "dom"),
            P(None, "dom"),
            P("dom", None),
            P("dom"),
            P(),
        ),
        out_specs=P("dom", None, None),
        check_vma=False,
    )
```
